32 devices in a mesh: groups: 2 (over x), leaf: 16 (over z, y, core).
Axes of the slice: x: 2, y: 2, z: 4, core: 2. Of those that a mesh axis runs over, the one named last changes fastest.
Arguments:
- right_side: float32 [256, 65536], P('groups', 'leaf'), parts along dimension 0, may hold values from -30 to 30
- point_order: int32 [131072], P(('groups', 'leaf')), parts along dimension 0, may hold values from 0 to 65535, as said below
- leaf_blocks: bfloat16 [128, 512, 512], P('leaf'), may hold values from -0.01 to 6, as said below
- bases: bfloat16 [7, 128, 65536], P(None, None, 'leaf'), may hold values from -4 to 4
- rank_weights: float32 [7, 128], replicated, may hold values from 0.05 to 0.6
Outputs:
- field_solution: float32 [256, 65536], P('groups', 'leaf'), parts along dimension 0
- field_residual: float32 [256, 65536], P('groups', 'leaf'), parts along dimension 0
The draws below stay inside these ranges and needn't reach their ends.
There are 2 independent parts, one for each index of `groups`. The reference program is written for one: setup_inputs(seed, part) draws one part's arguments, and reference() takes and returns one part's arrays. A program takes and returns all parts, laid end to end along the dimension named above; an argument that names none is the same for every part. Nothing has to cross between parts.
Inputs may be any that keep to these rules, and one draw needn't show every extreme that they name: `point_order`: each aligned run of 4096 entries holds each of its own 4096 positions once. `leaf_blocks`: every block is symmetric positive definite.
All inputs are finite; a program needn't handle non-finite values.
Results may differ from the reference program's by a relative error of at most 0.0049.
Values sent between devices are 32-bit elements; how exact they have to be, the bound alone decides.
A program may use at most 128 MiB of HBM per device.

```python
import math
import jax
import jax.numpy as jnp
from jax import lax

LEAF = 512
RANK = 128
NRHS = 128
ITERS = 2
PTS_DEV = 4096
PTS = 65536
BLOCKS = 128
LEVELS = 7


def draw_right_side(key, part):
    key_points, key_columns, key_values = jax.random.split(key, 3)
    position = jnp.arange(PTS, dtype=jnp.float32) / PTS
    trend = 1.0 + 2.0 * position
    point_scale = jnp.exp(jax.random.uniform(key_points, (PTS,), jnp.float32, 0.0, math.log(10.0)))
    values = jnp.clip(jax.random.normal(key_values, (NRHS, PTS), jnp.float32), -3.0, 3.0)
    column_scale = jnp.exp(jax.random.uniform(key_columns, (NRHS, 1), jnp.float32, 0.0, math.log(3.0)))
    return 0.1 * values * trend[None, :] * point_scale[None, :] * column_scale


def draw_point_order(key, part):
    device_count = PTS // PTS_DEV
    keys = jax.random.split(key, device_count)
    shuffled = jax.vmap(lambda single_key: jax.random.permutation(single_key, PTS_DEV))(keys)
    offsets = jnp.arange(device_count, dtype=jnp.int32)[:, None] * PTS_DEV
    return (shuffled.astype(jnp.int32) + offsets).reshape(PTS)


def leaf_kernel(block_key):
    key_spots, key_length, key_amplitude, key_rough, key_noise, key_nugget = jax.random.split(block_key, 6)
    counter = jnp.arange(LEAF, dtype=jnp.float32)
    spots = counter + jax.random.uniform(key_spots, (LEAF,), jnp.float32, 0.0, 0.9)
    length = jnp.exp(jax.random.uniform(key_length, (), jnp.float32, math.log(2.0), math.log(24.0)))
    amplitude = jax.random.uniform(key_amplitude, (), jnp.float32, 0.5, 1.5)
    roughness = jax.random.uniform(key_rough, (LEAF,), jnp.float32, 0.6, 1.4)
    jitter_noise = jax.random.uniform(key_noise, (LEAF, LEAF), jnp.float32, -0.004, 0.004)
    jitter_noise = 0.5 * (jitter_noise + jnp.transpose(jitter_noise))
    nugget = jax.random.uniform(key_nugget, (), jnp.float32, 2.2, 3.0)
    distance = jnp.abs(spots[:, None] - spots[None, :])
    kernel = amplitude * roughness[:, None] * roughness[None, :] * jnp.exp(-distance / length)
    identity = (counter[:, None] == counter[None, :]).astype(jnp.float32)
    return kernel + jitter_noise + nugget * identity


def draw_leaf_blocks(key, part):
    keys = jax.random.split(key, BLOCKS)
    return lax.map(leaf_kernel, keys).astype(jnp.bfloat16)


def block_scale(own_key, dims, cuts, low, largest):
    def one(axis_at, shards_of):
        heights = jax.random.uniform(jax.random.fold_in(jax.random.fold_in(own_key, 6), axis_at), (shards_of,), jnp.float32, low / len(cuts), largest / len(cuts))
        return jnp.repeat(jnp.exp(heights), dims[axis_at] // shards_of).reshape((-1,) + (1,) * (len(dims) - axis_at - 1))

    gain = one(*cuts[0])
    for cut in cuts[1:]:
        gain = gain * one(*cut)
    return gain


def scatter_about(stream_key, dims, scale, bound, cuts=(), held_as=jnp.bfloat16):
    values = jax.random.normal(stream_key, dims, jnp.float32) * scale
    if len(cuts) > 0:
        values = block_scale(stream_key, dims, cuts, -0.22, 0.18) * values
    return jnp.clip(values, min=-bound, max=bound).astype(held_as)


def setup_inputs(seed: int = 0, part: int = 0) -> dict:
    seeds = jax.random.split(jax.random.key(seed), 6)
    part_keys = jax.random.split(jax.random.fold_in(seeds[5], part), 6)
    right_side = draw_right_side(jax.random.fold_in(jax.random.fold_in(seeds[5], part), 71), part)
    point_order = draw_point_order(jax.random.fold_in(jax.random.fold_in(seeds[5], part), 71), part)
    leaf_blocks = draw_leaf_blocks(jax.random.fold_in(seeds[5], 71), part)
    bases = scatter_about(seeds[3], (LEVELS, RANK, PTS), 1.0, 4.0, ((2, 16),))
    rank_weights = jnp.clip(jnp.exp(jax.random.uniform(seeds[4], (LEVELS, RANK), jnp.float32, math.log(0.05), math.log(0.6))), 0.05, 0.6)
    return {"right_side": right_side, "point_order": point_order, "leaf_blocks": leaf_blocks, "bases": bases, "rank_weights": rank_weights}


def apply_operator(probe, leaf_blocks, bases, rank_weights):
    columns = probe.shape[0]
    indices = jnp.arange(BLOCKS, dtype=jnp.int32)

    def project(block_index):
        first_point = block_index * LEAF
        probe_piece = lax.dynamic_slice_in_dim(probe, first_point, LEAF, 1).astype(jnp.float32)
        basis_piece = lax.dynamic_slice_in_dim(bases, first_point, LEAF, 2).astype(jnp.float32)
        return jnp.einsum('np,lrp->lnr', probe_piece, basis_piece)
    partial_value = lax.map(project, indices)
    scaled_levels = []
    for tree_level in range(LEVELS):
        per_node = 2 ** (tree_level + 1)
        grouped = partial_value[:, tree_level].reshape(BLOCKS // per_node, per_node, columns, RANK).sum(axis=1)
        factor = 1.0 / math.sqrt(RANK * LEAF * per_node)
        scaled = (grouped * factor * rank_weights[tree_level]).astype(jnp.bfloat16)
        scaled_levels.append(jnp.repeat(scaled, per_node, axis=0))
    stacked = jnp.stack(scaled_levels, axis=1)

    def expand(operands):
        block_index, coefficients, leaf_block = operands
        first_point = block_index * LEAF
        probe_piece = lax.dynamic_slice_in_dim(probe, first_point, LEAF, 1)
        basis_piece = lax.dynamic_slice_in_dim(bases, first_point, LEAF, 2)
        dense_part = jnp.dot(probe_piece, leaf_block, preferred_element_type=jnp.float32)
        low_rank = jnp.einsum('lnr,lrp->np', coefficients.astype(jnp.float32), basis_piece.astype(jnp.float32))
        return dense_part + low_rank
    pieces = lax.map(expand, (indices, stacked, leaf_blocks))
    return pieces.transpose(1, 0, 2).reshape(columns, BLOCKS * LEAF)

def reference(right_side, point_order, leaf_blocks, bases, rank_weights):
    ordered = jnp.take(right_side, point_order, axis=1)
    solution = jnp.zeros_like(ordered)
    residual = ordered
    direction = ordered
    norm_now = lax.optimization_barrier(jnp.sum(residual * residual, axis=1))
    for iteration in range(ITERS):
        image_field = apply_operator(direction.astype(jnp.bfloat16), leaf_blocks, bases, rank_weights)
        step_size = norm_now / lax.optimization_barrier(jnp.sum(direction * image_field, axis=1))
        solution = solution + step_size[:, None] * direction
        residual = residual - step_size[:, None] * image_field
        if iteration + 1 < ITERS:
            norm_next = lax.optimization_barrier(jnp.sum(residual * residual, axis=1))
            direction = residual + (norm_next / norm_now)[:, None] * direction
            norm_now = norm_next
    field_solution = jnp.zeros_like(solution).at[:, point_order].set(solution)
    field_residual = jnp.zeros_like(residual).at[:, point_order].set(residual)
    return (field_solution, field_residual)
```

```python
import functools
import math

import jax
import jax.numpy as jnp
from jax import lax
from jax.experimental import pallas as pl
from jax.experimental.pallas import tpu as pltpu
from jax.sharding import PartitionSpec as P

ITERS = 2
TILE = 128
MESH = pl.DeviceIdType.MESH


def nt_dot(a, b):
    return lax.dot_general(a, b, (((1,), (1,)), ((), ())), preferred_element_type=jnp.float32)


def nn_dot(a, b):
    return jnp.dot(a, b, preferred_element_type=jnp.float32)


def row_of(matrix):
    return jnp.sum(matrix.T, axis=0, keepdims=True)


def spread(row):
    return jnp.broadcast_to(row, (TILE, row.shape[1])).T


def cg_kernel(n_dev, levels, *refs):
    upper = n_dev.bit_length() - 1
    local = levels - upper
    rs_hbm, order_ref, leaf_hbm, bases_hbm, weights_ref, sol_ref, res_ref = refs[:7]
    (rs, rst, rows, leaf, bases, dirn, probe, image, coef, low_s, up_s, pend0, recv_a, recv_b, total,
     vec_out, vec_in) = refs[7:24]
    pends = refs[24:24 + upper - 1]
    recvs = refs[24 + upper - 1:24 + 2 * (upper - 1)]
    rs_sem, leaf_sem, bases_sem, send_sem, recv_sem, vsend_sem, vrecv_sem = refs[24 + 2 * (upper - 1):]

    columns, points = rs.shape
    blocks, leaf_size = leaf.shape[0], leaf.shape[1]
    tiles = points // TILE
    half = columns // 2
    me = lax.axis_index("leaf")
    core = me % 2

    rs_copy = pltpu.make_async_copy(rs_hbm, rs, rs_sem)
    rs_copy.start()
    bases_copy = pltpu.make_async_copy(bases_hbm, bases, bases_sem)
    bases_copy.start()
    leaf_copy = pltpu.make_async_copy(leaf_hbm, leaf, leaf_sem)
    leaf_copy.start()

    barrier = pltpu.get_barrier_semaphore()

    def greet(k, carry):
        pl.semaphore_signal(
            barrier, inc=1, device_id={"leaf": (me + k) % n_dev}, device_id_type=MESH
        )
        return carry

    lax.fori_loop(1, n_dev, greet, 0)

    rs_copy.wait()

    def turn(c, carry):
        at = pl.multiple_of(c * TILE, TILE)
        rst[pl.ds(at, TILE), :] = rs[:, pl.ds(at, TILE)].T
        return carry

    lax.fori_loop(0, tiles, turn, 0)

    def fetch(c, carry):
        at = pl.multiple_of(c * TILE, TILE)
        for j in range(TILE):
            source = order_ref[at + j] & (points - 1)
            rows[pl.ds(j, 1), :] = rst[pl.ds(source, 1), :]
        picked = rows[...].T
        dirn[:, pl.ds(at, TILE)] = picked
        probe[:, pl.ds(at, TILE)] = picked.astype(jnp.bfloat16)
        return carry

    lax.fori_loop(0, tiles, fetch, 0)

    def partner(bit):
        stride = 2 ** bit
        return me + stride * (1 - 2 * ((me // stride) % 2))

    def send(source, target, it, slot, bit):
        copy = pltpu.make_async_remote_copy(
            src_ref=source,
            dst_ref=target,
            send_sem=send_sem.at[it, slot],
            recv_sem=recv_sem.at[it, slot],
            device_id={"leaf": partner(bit)},
            device_id_type=MESH,
        )
        copy.start()
        return copy

    def scaled(values, level):
        factor = 1.0 / math.sqrt(columns_rank * leaf_size * 2 ** (level + 1))
        return (values * factor * weights_ref[level:level + 1, :]).astype(jnp.bfloat16)

    columns_rank = weights_ref.shape[1]
    rank = columns_rank
    mine = pl.ds(pl.multiple_of(core * half, half), half)
    theirs = pl.ds(pl.multiple_of((1 - core) * half, half), half)
    low = local * rank
    bases_copy.wait()

    for it in range(ITERS):
        up = nt_dot(probe[...], bases[low:, :])
        for u in range(upper):
            pend0[it, u] = up[:, u * rank:(u + 1) * rank]
        if it == 0:
            pl.semaphore_wait(barrier, n_dev - 1)
        whole_copy = send(pend0.at[it, 0], recv_a.at[it], it, 0, 0)
        half_copy = send(pend0.at[it, pl.ds(1, upper - 1), theirs], recv_b.at[it], it, 1, 0)
        sent = [whole_copy, half_copy]
        back = []
        state = {"round": 0, "copy": None}

        def advance():
            t = state["round"]
            if t >= upper:
                return
            if t == 0:
                whole_copy.wait_recv()
                half_copy.wait_recv()
                total[it, 0] = pend0[it, 0] + recv_a[it]
                pends[0][it] = pend0[it, pl.ds(1, upper - 1), mine] + recv_b[it]
            else:
                state["copy"].wait_recv()
                total[it, t, mine] = pends[t - 1][it, 0] + recvs[t - 1][it, 0]
                gather = send(total.at[it, t, mine], total.at[it, t, mine], it, upper + t, 0)
                back.append(gather)
                sent.append(gather)
                if t + 1 < upper:
                    pends[t][it] = pends[t - 1][it, 1:] + recvs[t - 1][it, 1:]
            if t + 1 < upper:
                state["copy"] = send(pends[t].at[it], recvs[t].at[it], it, 2 + t, t + 1)
                sent.append(state["copy"])
            state["round"] = t + 1

        for b in range(blocks):
            span = slice(b * leaf_size, (b + 1) * leaf_size)
            coef[b] = nt_dot(probe[:, span], bases[:low, span])
        for level in range(local):
            per_node = 2 ** (level + 1)
            lanes = slice(level * rank, (level + 1) * rank)
            for q in range(blocks // per_node):
                node = coef[q * per_node, :, lanes]
                for b in range(q * per_node + 1, (q + 1) * per_node):
                    node = node + coef[b, :, lanes]
                value = scaled(node, level)
                for b in range(q * per_node, (q + 1) * per_node):
                    low_s[b, :, lanes] = value
        advance()
        if it == 0:
            leaf_copy.wait()
        for b in range(blocks):
            span = slice(b * leaf_size, (b + 1) * leaf_size)
            image[:, span] = nn_dot(probe[:, span], leaf[b]) + nn_dot(low_s[b], bases[:low, span])
            if b % 4 == 3:
                advance()
        for _ in range(upper):
            advance()
        for copy in back:
            copy.wait_recv()
        for u in range(upper):
            up_s[:, u * rank:(u + 1) * rank] = scaled(total[it, u], local + u)

        curve = jnp.zeros((columns, TILE), jnp.float32)
        norm = jnp.zeros((columns, TILE), jnp.float32)
        power = jnp.zeros((columns, TILE), jnp.float32)
        held = dirn if it == 0 else res_ref
        for b in range(blocks):
            span = slice(b * leaf_size, (b + 1) * leaf_size)
            field = image[:, span] + nn_dot(up_s[...], bases[low:, span])
            image[:, span] = field
            for c in range(leaf_size // TILE):
                at = b * leaf_size + c * TILE
                piece = field[:, c * TILE:(c + 1) * TILE]
                away = dirn[:, at:at + TILE]
                curve = curve + away * piece
                left = held[:, at:at + TILE]
                norm = norm + left * left
                if it + 1 < ITERS:
                    power = power + piece * piece
        vec_out[it, 0:1, :] = row_of(curve)
        vec_out[it, 1:2, :] = row_of(norm)
        vec_out[it, 2:3, :] = row_of(power)
        vec_out[it, 3:8, :] = jnp.zeros((5, TILE), jnp.float32)

        def vector(k):
            return pltpu.make_async_remote_copy(
                src_ref=vec_out.at[it],
                dst_ref=vec_in.at[it, k],
                send_sem=vsend_sem.at[it, k],
                recv_sem=vrecv_sem.at[it, k],
                device_id={"leaf": (me + k) % n_dev},
                device_id_type=MESH,
            )

        def push(k, carry):
            vector(k).start()
            return carry

        def take(k, carry):
            vector(k).wait()
            return carry + vec_in[it, k]

        lax.fori_loop(1, n_dev, push, 0)
        for copy in sent:
            copy.wait_send()
        sums = lax.fori_loop(1, n_dev, take, vec_out[it])
        curvature, norm_now, squares = sums[0:1], sums[1:2], sums[2:3]
        step_row = norm_now / curvature
        step = spread(step_row)
        if it + 1 < ITERS:
            norm_next = norm_now - 2.0 * step_row * curvature + step_row * step_row * squares
            ratio = spread(norm_next / norm_now)

        def update(c, carry):
            lanes = pl.ds(pl.multiple_of(c * TILE, TILE), TILE)
            away = dirn[:, lanes]
            if it == 0:
                sol_ref[:, lanes] = step * away
                left = away - step * image[:, lanes]
            else:
                sol_ref[:, lanes] = sol_ref[:, lanes] + step * away
                left = res_ref[:, lanes] - step * image[:, lanes]
            res_ref[:, lanes] = left
            if it + 1 < ITERS:
                fresh = left + ratio * away
                dirn[:, lanes] = fresh
                probe[:, lanes] = fresh.astype(jnp.bfloat16)
            return carry

        lax.fori_loop(0, tiles, update, 0)


def conjugate(right_side, point_order, leaf_blocks, bases, rank_weights, n_dev):
    columns, points = right_side.shape
    blocks, leaf_size, _ = leaf_blocks.shape
    levels, rank = rank_weights.shape
    upper = n_dev.bit_length() - 1
    local = levels - upper
    half = columns // 2
    f32, bf16 = jnp.float32, jnp.bfloat16
    scratch = [
        pltpu.VMEM((columns, points), f32),
        pltpu.VMEM((points, columns), f32),
        pltpu.VMEM((TILE, columns), f32),
        pltpu.VMEM((blocks, leaf_size, leaf_size), bf16),
        pltpu.VMEM((levels * rank, points), bf16),
        pltpu.VMEM((columns, points), f32),
        pltpu.VMEM((columns, points), bf16),
        pltpu.VMEM((columns, points), f32),
        pltpu.VMEM((blocks, columns, local * rank), f32),
        pltpu.VMEM((blocks, columns, local * rank), bf16),
        pltpu.VMEM((columns, upper * rank), bf16),
        pltpu.VMEM((ITERS, upper, columns, rank), f32),
        pltpu.VMEM((ITERS, columns, rank), f32),
        pltpu.VMEM((ITERS, upper - 1, half, rank), f32),
        pltpu.VMEM((ITERS, upper, columns, rank), f32),
        pltpu.VMEM((ITERS, 8, columns), f32),
        pltpu.VMEM((ITERS, n_dev, 8, columns), f32),
    ]
    rounds = [pltpu.VMEM((ITERS, upper - t, half, rank), f32) for t in range(1, upper)]
    scratch += rounds + rounds
    scratch += [
        pltpu.SemaphoreType.DMA,
        pltpu.SemaphoreType.DMA,
        pltpu.SemaphoreType.DMA,
        pltpu.SemaphoreType.DMA((ITERS, 2 * upper)),
        pltpu.SemaphoreType.DMA((ITERS, 2 * upper)),
        pltpu.SemaphoreType.DMA((ITERS, n_dev)),
        pltpu.SemaphoreType.DMA((ITERS, n_dev)),
    ]
    hbm = pl.BlockSpec(memory_space=pl.ANY)
    vmem = pl.BlockSpec(memory_space=pltpu.VMEM)
    shape = jax.ShapeDtypeStruct((columns, points), f32)
    return pl.pallas_call(
        functools.partial(cg_kernel, n_dev, levels),
        out_shape=(shape, shape),
        in_specs=[hbm, pl.BlockSpec(memory_space=pltpu.SMEM), hbm, hbm, vmem],
        out_specs=(vmem, vmem),
        scratch_shapes=scratch,
        compiler_params=pltpu.CompilerParams(
            collective_id=0, has_side_effects=True, vmem_limit_bytes=56 * 2 ** 20
        ),
        name="cg",
    )(right_side, point_order, leaf_blocks, bases.reshape(levels * rank, points), rank_weights)


def scatter_kernel(order_ref, sol_ref, res_ref, out_sol, out_res, sol_rows, res_rows, sol_tile, res_tile):
    columns, points = sol_ref.shape
    tiles = points // TILE

    def place(c, carry):
        at = pl.multiple_of(c * TILE, TILE)
        sol_tile[...] = sol_ref[:, pl.ds(at, TILE)].T
        res_tile[...] = res_ref[:, pl.ds(at, TILE)].T
        for j in range(TILE):
            target = order_ref[at + j] & (points - 1)
            sol_rows[pl.ds(target, 1), :] = sol_tile[pl.ds(j, 1), :]
            res_rows[pl.ds(target, 1), :] = res_tile[pl.ds(j, 1), :]
        return carry

    lax.fori_loop(0, tiles, place, 0)

    def turn(c, carry):
        at = pl.multiple_of(c * TILE, TILE)
        out_sol[:, pl.ds(at, TILE)] = sol_rows[pl.ds(at, TILE), :].T
        out_res[:, pl.ds(at, TILE)] = res_rows[pl.ds(at, TILE), :].T
        return carry

    lax.fori_loop(0, tiles, turn, 0)


def scatter_back(point_order, field, residual):
    columns, points = field.shape
    vmem = pl.BlockSpec(memory_space=pltpu.VMEM)
    shape = jax.ShapeDtypeStruct((columns, points), jnp.float32)
    return pl.pallas_call(
        scatter_kernel,
        out_shape=(shape, shape),
        in_specs=[pl.BlockSpec(memory_space=pltpu.SMEM), vmem, vmem],
        out_specs=(vmem, vmem),
        scratch_shapes=[
            pltpu.VMEM((points, columns), jnp.float32),
            pltpu.VMEM((points, columns), jnp.float32),
            pltpu.VMEM((TILE, columns), jnp.float32),
            pltpu.VMEM((TILE, columns), jnp.float32),
        ],
        compiler_params=pltpu.CompilerParams(vmem_limit_bytes=40 * 2 ** 20),
        name="place",
    )(point_order, field, residual)


def on_device(right_side, point_order, leaf_blocks, bases, rank_weights, n_dev):
    field, residual = conjugate(right_side, point_order, leaf_blocks, bases, rank_weights, n_dev)
    return scatter_back(point_order, field, residual)


def solution(mesh):
    return jax.shard_map(
        functools.partial(on_device, n_dev=mesh.shape["leaf"]),
        mesh=mesh,
        in_specs=(
            P("groups", "leaf"),
            P(("groups", "leaf")),
            P("leaf", None, None),
            P(None, None, "leaf"),
            P(),
        ),
        out_specs=(P("groups", "leaf"), P("groups", "leaf")),
        check_vma=False,
    )
```

```python
import functools
import math

import jax
import jax.numpy as jnp
from jax import lax
from jax.experimental import pallas as pl
from jax.experimental.pallas import tpu as pltpu
from jax.sharding import PartitionSpec as P

ITERS = 2
TILE = 128
CHUNKS = 4
MESH = pl.DeviceIdType.MESH


def nt_dot(a, b):
    return lax.dot_general(a, b, (((1,), (1,)), ((), ())), preferred_element_type=jnp.float32)


def nn_dot(a, b):
    return jnp.dot(a, b, preferred_element_type=jnp.float32)


def row_of(matrix):
    return jnp.sum(matrix.T, axis=0, keepdims=True)


def spread(row):
    return jnp.broadcast_to(row, (TILE, row.shape[1])).T


def cg_kernel(n_dev, levels, n_stage, *refs):
    upper = n_dev.bit_length() - 1
    local = levels - upper
    refs = list(refs)

    def grab(count):
        taken = refs[:count]
        del refs[:count]
        return taken

    rs_hbm, order_ref, leaf_hbm, bases_hbm, weights_ref, sol_hbm, res_hbm = grab(7)
    rs, rst, rows, srows, leaf, bases, dirn, left_field, probe, image, coef, low_s, up_s = grab(13)
    pend0, recv_a, recv_q, total, vec_out, vec_in = grab(6)
    pends, firsts, others = grab(n_stage), grab(n_stage), grab(n_stage)
    rs_sem, leaf_sem, bases_sem, send_sem, recv_sem, vsend_sem, vrecv_sem, out_sem = grab(8)

    columns, points = rs.shape
    blocks, leaf_size = leaf.shape[0], leaf.shape[1]
    rank = weights_ref.shape[1]
    tiles = points // TILE
    quarter = columns // 4
    me = lax.axis_index("leaf")

    part = points // CHUNKS
    rs_copies = []
    for q in range(CHUNKS):
        lanes = pl.ds(q * part, part)
        copy = pltpu.make_async_copy(rs_hbm.at[:, lanes], rs.at[:, lanes], rs_sem.at[q])
        copy.start()
        rs_copies.append(copy)
    bases_copy = pltpu.make_async_copy(bases_hbm, bases, bases_sem)
    bases_copy.start()
    leaf_copy = pltpu.make_async_copy(leaf_hbm, leaf, leaf_sem)
    leaf_copy.start()

    barrier = pltpu.get_barrier_semaphore()

    def greet(k, carry):
        pl.semaphore_signal(
            barrier, inc=1, device_id={"leaf": (me + k) % n_dev}, device_id_type=MESH
        )
        return carry

    lax.fori_loop(1, n_dev, greet, 0)

    for q in range(CHUNKS):
        rs_copies[q].wait()
        for c in range(q * tiles // CHUNKS, (q + 1) * tiles // CHUNKS):
            at = c * TILE
            rst[at:at + TILE, :] = rs[:, at:at + TILE].T

    def fetch(at):
        for j in range(TILE):
            source = order_ref[at + j] & (points - 1)
            rows[pl.ds(j, 1), :] = rst[pl.ds(source, 1), :]

    def keep(at, tile):
        picked = tile.T
        dirn[:, pl.ds(at, TILE)] = picked
        probe[:, pl.ds(at, TILE)] = picked.astype(jnp.bfloat16)

    def fetch_keep(c, carry):
        at = pl.multiple_of(c * TILE, TILE)
        before = rows[...]
        fetch(at)
        keep(pl.multiple_of(at - TILE, TILE), before)
        return carry

    fetch(0)
    lax.fori_loop(1, tiles, fetch_keep, 0)
    keep(points - TILE, rows[...])

    def flip(k, bit):
        peer = me
        for step in range(2):
            if k >> step & 1:
                stride = 2 ** (bit + step)
                peer = peer + stride * (1 - 2 * ((me // stride) % 2))
        return peer

    def quarter_of(device):
        return pl.ds(pl.multiple_of(device % 4 * quarter, quarter), quarter)

    def scaled(values, level):
        factor = 1.0 / math.sqrt(rank * leaf_size * 2 ** (level + 1))
        return (values * factor * weights_ref[level:level + 1, :]).astype(jnp.bfloat16)

    mine = quarter_of(me)
    low = local * rank
    bases_copy.wait()

    for it in range(ITERS):
        up = nt_dot(probe[...], bases[low:, :])
        for u in range(upper):
            pend0[it, u] = up[:, u * rank:(u + 1) * rank]
        if it == 0:
            pl.semaphore_wait(barrier, n_dev - 1)
        sent = []

        def send(source, target, k, bit):
            slot = len(sent)
            copy = pltpu.make_async_remote_copy(
                src_ref=source,
                dst_ref=target,
                send_sem=send_sem.at[it, slot],
                recv_sem=recv_sem.at[it, slot],
                device_id={"leaf": flip(k, bit)},
                device_id_type=MESH,
            )
            copy.start()
            sent.append(copy)
            return copy

        def share(first, count):
            place = total.at[it, pl.ds(first, count), mine]
            return [send(place, place, k, 0) for k in (3, 2, 1)]

        def launch(stage):
            bit = 2 * stage + 2
            count = upper - bit
            copies = [send(pends[stage].at[it], firsts[stage].at[it], 1, bit)]
            if count > 1:
                for k in (2, 3):
                    copies.append(send(
                        pends[stage].at[it, pl.ds(1, count - 1)],
                        others[stage].at[it, k - 2], k, bit))
            return copies

        opening = [
            send(pend0.at[it, pl.ds(1, upper - 1), quarter_of(flip(k, 0))],
                 recv_q.at[it, k - 1], k, 0)
            for k in (3, 2, 1)
        ]
        opening.append(send(pend0.at[it, 0], recv_a.at[it], 1, 0))
        state = {"round": 0, "copies": opening, "back": []}

        def advance():
            stage = state["round"] - 1
            if stage >= n_stage:
                return
            for copy in state["copies"]:
                copy.wait_recv()
            if stage < 0:
                for u in range(1, upper):
                    value = pend0[it, u, mine]
                    for k in range(3):
                        value = value + recv_q[it, k, u - 1]
                    if u == 1:
                        total[it, u, mine] = value
                    else:
                        pends[0][it, u - 2] = value
                if n_stage > 0:
                    state["copies"] = launch(0)
                state["back"] += share(1, 1)
                total[it, 0] = pend0[it, 0] + recv_a[it]
            else:
                bit = 2 * stage + 2
                for u in range(bit, upper):
                    value = pends[stage][it, u - bit] + firsts[stage][it, u - bit]
                    if u > bit:
                        for k in range(2):
                            value = value + others[stage][it, k, u - bit - 1]
                    if u < bit + 2:
                        total[it, u, mine] = value
                    else:
                        pends[stage + 1][it, u - bit - 2] = value
                if stage + 1 < n_stage:
                    state["copies"] = launch(stage + 1)
                state["back"] += share(bit, min(2, upper - bit))
            state["round"] += 1

        for b in range(blocks):
            span = slice(b * leaf_size, (b + 1) * leaf_size)
            coef[b] = nt_dot(probe[:, span], bases[:low, span])
        for level in range(local):
            per_node = 2 ** (level + 1)
            lanes = slice(level * rank, (level + 1) * rank)
            for q in range(blocks // per_node):
                node = coef[q * per_node, :, lanes]
                for b in range(q * per_node + 1, (q + 1) * per_node):
                    node = node + coef[b, :, lanes]
                value = scaled(node, level)
                for b in range(q * per_node, (q + 1) * per_node):
                    low_s[b, :, lanes] = value
        if it == 0:
            leaf_copy.wait()
        for b in range(blocks):
            span = slice(b * leaf_size, (b + 1) * leaf_size)
            image[:, span] = nn_dot(probe[:, span], leaf[b]) + nn_dot(low_s[b], bases[:low, span])
            if b == blocks - 3:
                advance()
        for _ in range(n_stage):
            advance()
        for copy in state["back"]:
            copy.wait_recv()
        for u in range(upper):
            up_s[:, u * rank:(u + 1) * rank] = scaled(total[it, u], local + u)

        curve = jnp.zeros((columns, TILE), jnp.float32)
        norm = jnp.zeros((columns, TILE), jnp.float32)
        power = jnp.zeros((columns, TILE), jnp.float32)
        held = dirn if it == 0 else left_field
        for b in range(blocks):
            span = slice(b * leaf_size, (b + 1) * leaf_size)
            field = image[:, span] + nn_dot(up_s[...], bases[low:, span])
            image[:, span] = field
            for c in range(leaf_size // TILE):
                at = b * leaf_size + c * TILE
                piece = field[:, c * TILE:(c + 1) * TILE]
                away = dirn[:, at:at + TILE]
                curve = curve + away * piece
                left = held[:, at:at + TILE]
                norm = norm + left * left
                if it + 1 < ITERS:
                    power = power + piece * piece
        vec_out[it, 0, 0:1, :] = row_of(curve)
        vec_out[it, 0, 1:2, :] = row_of(norm)
        vec_out[it, 0, 2:3, :] = row_of(power)
        vec_out[it, 0, 3:8, :] = jnp.zeros((5, TILE), jnp.float32)
        for stage in range(n_stage + 1):
            bit = 2 * stage
            peers = (3, 2, 1) if bit + 1 < upper else (1,)
            hops = []
            for k in peers:
                slot = stage * 3 + k - 1
                hop = pltpu.make_async_remote_copy(
                    src_ref=vec_out.at[it, stage],
                    dst_ref=vec_in.at[it, slot],
                    send_sem=vsend_sem.at[it, slot],
                    recv_sem=vrecv_sem.at[it, slot],
                    device_id={"leaf": flip(k, bit)},
                    device_id_type=MESH,
                )
                hop.start()
                hops.append(hop)
            if stage == 0:
                for copy in sent:
                    copy.wait_send()
            sums = vec_out[it, stage]
            for hop, k in zip(hops, peers):
                hop.wait()
                sums = sums + vec_in[it, stage * 3 + k - 1]
            if stage < n_stage:
                vec_out[it, stage + 1] = sums
        curvature, norm_now, squares = sums[0:1], sums[1:2], sums[2:3]
        step_row = norm_now / curvature
        step = spread(step_row)
        if it + 1 < ITERS:
            norm_next = norm_now - 2.0 * step_row * curvature + step_row * step_row * squares
            ratio = spread(norm_next / norm_now)
            for c in range(tiles):
                lanes = slice(c * TILE, (c + 1) * TILE)
                away = dirn[:, lanes]
                if it == 0:
                    rs[:, lanes] = step * away
                    left = away - step * image[:, lanes]
                else:
                    rs[:, lanes] = rs[:, lanes] + step * away
                    left = left_field[:, lanes] - step * image[:, lanes]
                left_field[:, lanes] = left
                fresh = left + ratio * away
                dirn[:, lanes] = fresh
                probe[:, lanes] = fresh.astype(jnp.bfloat16)

    outs = []
    for q in range(CHUNKS):
        for c in range(q * tiles // CHUNKS, (q + 1) * tiles // CHUNKS):
            lanes = slice(c * TILE, (c + 1) * TILE)
            srows[lanes, :] = (rs[:, lanes] + step * dirn[:, lanes]).T
            rst[lanes, :] = (left_field[:, lanes] - step * image[:, lanes]).T
        run = pl.ds(q * part, part)
        for n, (source, target) in enumerate(((srows, sol_hbm), (rst, res_hbm))):
            copy = pltpu.make_async_copy(source.at[run], target.at[run], out_sem.at[n, q])
            copy.start()
            outs.append(copy)
    for copy in outs:
        copy.wait()


def conjugate(right_side, point_order, leaf_blocks, bases, rank_weights, n_dev):
    columns, points = right_side.shape
    blocks, leaf_size, _ = leaf_blocks.shape
    levels, rank = rank_weights.shape
    upper = n_dev.bit_length() - 1
    local = levels - upper
    quarter = columns // 4
    starts = list(range(2, upper, 2))
    n_stage = len(starts)
    f32, bf16 = jnp.float32, jnp.bfloat16
    scratch = [
        pltpu.VMEM((columns, points), f32),
        pltpu.VMEM((points, columns), f32),
        pltpu.VMEM((TILE, columns), f32),
        pltpu.VMEM((points, columns), f32),
        pltpu.VMEM((blocks, leaf_size, leaf_size), bf16),
        pltpu.VMEM((levels * rank, points), bf16),
        pltpu.VMEM((columns, points), f32),
        pltpu.VMEM((columns, points), f32),
        pltpu.VMEM((columns, points), bf16),
        pltpu.VMEM((columns, points), f32),
        pltpu.VMEM((blocks, columns, local * rank), f32),
        pltpu.VMEM((blocks, columns, local * rank), bf16),
        pltpu.VMEM((columns, upper * rank), bf16),
        pltpu.VMEM((ITERS, upper, columns, rank), f32),
        pltpu.VMEM((ITERS, columns, rank), f32),
        pltpu.VMEM((ITERS, 3, upper - 1, quarter, rank), f32),
        pltpu.VMEM((ITERS, upper, columns, rank), f32),
        pltpu.VMEM((ITERS, n_stage + 1, 8, columns), f32),
        pltpu.VMEM((ITERS, 3 * (n_stage + 1), 8, columns), f32),
    ]
    scratch += [pltpu.VMEM((ITERS, upper - b, quarter, rank), f32) for b in starts]
    scratch += [pltpu.VMEM((ITERS, upper - b, quarter, rank), f32) for b in starts]
    scratch += [pltpu.VMEM((ITERS, 2, max(upper - b - 1, 1), quarter, rank), f32) for b in starts]
    slots = 7 + 6 * n_stage
    scratch += [
        pltpu.SemaphoreType.DMA((CHUNKS,)),
        pltpu.SemaphoreType.DMA,
        pltpu.SemaphoreType.DMA,
        pltpu.SemaphoreType.DMA((ITERS, slots)),
        pltpu.SemaphoreType.DMA((ITERS, slots)),
        pltpu.SemaphoreType.DMA((ITERS, 3 * (n_stage + 1))),
        pltpu.SemaphoreType.DMA((ITERS, 3 * (n_stage + 1))),
        pltpu.SemaphoreType.DMA((2, CHUNKS)),
    ]
    hbm = pl.BlockSpec(memory_space=pl.ANY)
    vmem = pl.BlockSpec(memory_space=pltpu.VMEM)
    shape = jax.ShapeDtypeStruct((points, columns), f32)
    return pl.pallas_call(
        functools.partial(cg_kernel, n_dev, levels, n_stage),
        out_shape=(shape, shape),
        in_specs=[hbm, pl.BlockSpec(memory_space=pltpu.SMEM), hbm, hbm, vmem],
        out_specs=(hbm, hbm),
        scratch_shapes=scratch,
        compiler_params=pltpu.CompilerParams(
            collective_id=0, has_side_effects=True, vmem_limit_bytes=56 * 2 ** 20
        ),
        name="cg",
    )(right_side, point_order, leaf_blocks, bases.reshape(levels * rank, points), rank_weights)


def scatter_kernel(order_ref, sol_hbm, res_hbm, out_sol, out_res, sol_in, res_in, sol_rows, res_rows,
                   sol_turn, res_turn, in_sem, out_sem):
    points, columns = sol_in.shape
    tiles = points // TILE
    part = points // CHUNKS
    copies = []
    for q in range(CHUNKS):
        run = pl.ds(q * part, part)
        pair = []
        for n, (source, target) in enumerate(((sol_hbm, sol_in), (res_hbm, res_in))):
            copy = pltpu.make_async_copy(source.at[run], target.at[run], in_sem.at[n, q])
            copy.start()
            pair.append(copy)
        copies.append(pair)

    def place(c, carry):
        at = pl.multiple_of(c * TILE, TILE)
        for j in range(TILE):
            target = order_ref[at + j] & (points - 1)
            sol_rows[pl.ds(target, 1), :] = sol_in[pl.ds(at + j, 1), :]
            res_rows[pl.ds(target, 1), :] = res_in[pl.ds(at + j, 1), :]
        return carry

    for q in range(CHUNKS):
        for copy in copies[q]:
            copy.wait()
        lax.fori_loop(q * tiles // CHUNKS, (q + 1) * tiles // CHUNKS, place, 0)

    outs = []
    for q in range(CHUNKS):
        for c in range(q * tiles // CHUNKS, (q + 1) * tiles // CHUNKS):
            lanes = slice(c * TILE, (c + 1) * TILE)
            sol_turn[:, lanes] = sol_rows[lanes, :].T
            res_turn[:, lanes] = res_rows[lanes, :].T
        run = pl.ds(q * part, part)
        for n, (source, target) in enumerate(((sol_turn, out_sol), (res_turn, out_res))):
            copy = pltpu.make_async_copy(source.at[:, run], target.at[:, run], out_sem.at[n, q])
            copy.start()
            outs.append(copy)
    for copy in outs:
        copy.wait()


def scatter_back(point_order, field, residual):
    points, columns = field.shape
    hbm = pl.BlockSpec(memory_space=pl.ANY)
    shape = jax.ShapeDtypeStruct((columns, points), jnp.float32)
    return pl.pallas_call(
        scatter_kernel,
        out_shape=(shape, shape),
        in_specs=[pl.BlockSpec(memory_space=pltpu.SMEM), hbm, hbm],
        out_specs=(hbm, hbm),
        scratch_shapes=[pltpu.VMEM((points, columns), jnp.float32)] * 4
        + [pltpu.VMEM((columns, points), jnp.float32)] * 2
        + [pltpu.SemaphoreType.DMA((2, CHUNKS))] * 2,
        compiler_params=pltpu.CompilerParams(vmem_limit_bytes=56 * 2 ** 20),
        name="place",
    )(point_order, field, residual)


def on_device(right_side, point_order, leaf_blocks, bases, rank_weights, n_dev):
    field, residual = conjugate(right_side, point_order, leaf_blocks, bases, rank_weights, n_dev)
    return scatter_back(point_order, field, residual)


def solution(mesh):
    return jax.shard_map(
        functools.partial(on_device, n_dev=mesh.shape["leaf"]),
        mesh=mesh,
        in_specs=(
            P("groups", "leaf"),
            P(("groups", "leaf")),
            P("leaf", None, None),
            P(None, None, "leaf"),
            P(),
        ),
        out_specs=(P("groups", "leaf"), P("groups", "leaf")),
        check_vma=False,
    )
```

```python
import functools
import math

import jax
import jax.numpy as jnp
from jax import lax
from jax.experimental import pallas as pl
from jax.experimental.pallas import tpu as pltpu
from jax.sharding import PartitionSpec as P

ITERS = 2
TILE = 128
CHUNKS = 4
MESH = pl.DeviceIdType.MESH


def nt_dot(a, b):
    return lax.dot_general(a, b, (((1,), (1,)), ((), ())), preferred_element_type=jnp.float32)


def nn_dot(a, b):
    return jnp.dot(a, b, preferred_element_type=jnp.float32)


def row_of(matrix):
    return jnp.sum(matrix.T, axis=0, keepdims=True)


def spread(row):
    return jnp.broadcast_to(row, (TILE, row.shape[1])).T


def cg_kernel(n_dev, levels, n_stage, *refs):
    upper = n_dev.bit_length() - 1
    local = levels - upper
    refs = list(refs)

    def grab(count):
        taken = refs[:count]
        del refs[:count]
        return taken

    rs_hbm, order_ref, leaf_hbm, bases_hbm, weights_ref, sol_hbm, res_hbm = grab(7)
    rs, rst, rows, srows, leaf, bases, dirn, left_field, probe, image, coef, low_s, up_s = grab(13)
    pend0, recv_a, recv_q, total, products, vec_out, vec_in = grab(7)
    pends, firsts, others = grab(n_stage), grab(n_stage), grab(n_stage)
    rs_sem, leaf_sem, bases_sem, send_sem, recv_sem, vsend_sem, vrecv_sem, out_sem = grab(8)

    columns, points = rs.shape
    blocks, leaf_size = leaf.shape[0], leaf.shape[1]
    rank = weights_ref.shape[1]
    tiles = points // TILE
    quarter = columns // 4
    me = lax.axis_index("leaf")

    part = points // CHUNKS
    rs_copies = []
    for q in range(CHUNKS):
        lanes = pl.ds(q * part, part)
        copy = pltpu.make_async_copy(rs_hbm.at[:, lanes], rs.at[:, lanes], rs_sem.at[q])
        copy.start()
        rs_copies.append(copy)
    bases_copy = pltpu.make_async_copy(bases_hbm, bases, bases_sem)
    bases_copy.start()
    leaf_copy = pltpu.make_async_copy(leaf_hbm, leaf, leaf_sem)
    leaf_copy.start()

    barrier = pltpu.get_barrier_semaphore()

    def greet(k, carry):
        pl.semaphore_signal(
            barrier, inc=1, device_id={"leaf": (me + k) % n_dev}, device_id_type=MESH
        )
        return carry

    lax.fori_loop(1, n_dev, greet, 0)

    for q in range(CHUNKS):
        rs_copies[q].wait()
        for c in range(q * tiles // CHUNKS, (q + 1) * tiles // CHUNKS):
            at = c * TILE
            rst[at:at + TILE, :] = rs[:, at:at + TILE].T

    def fetch(at):
        for j in range(TILE):
            source = order_ref[at + j] & (points - 1)
            rows[pl.ds(j, 1), :] = rst[pl.ds(source, 1), :]

    def keep(at, tile):
        picked = tile.T
        dirn[:, pl.ds(at, TILE)] = picked
        probe[:, pl.ds(at, TILE)] = picked.astype(jnp.bfloat16)

    def fetch_keep(c, carry):
        at = pl.multiple_of(c * TILE, TILE)
        before = rows[...]
        fetch(at)
        keep(pl.multiple_of(at - TILE, TILE), before)
        return carry

    fetch(0)
    lax.fori_loop(1, tiles, fetch_keep, 0)
    keep(points - TILE, rows[...])

    def flip(k, bit):
        peer = me
        for step in range(2):
            if k >> step & 1:
                stride = 2 ** (bit + step)
                peer = peer + stride * (1 - 2 * ((me // stride) % 2))
        return peer

    def quarter_of(device):
        return pl.ds(pl.multiple_of(device % 4 * quarter, quarter), quarter)

    def scaled(values, level):
        factor = 1.0 / math.sqrt(rank * leaf_size * 2 ** (level + 1))
        return (values * factor * weights_ref[level:level + 1, :]).astype(jnp.bfloat16)

    mine = quarter_of(me)
    low = local * rank
    bases_copy.wait()

    for it in range(ITERS):
        up = nt_dot(probe[...], bases[low:, :])
        for u in range(upper):
            pend0[it, u] = up[:, u * rank:(u + 1) * rank]
        if it == 0:
            pl.semaphore_wait(barrier, n_dev - 1)
        sent = []

        def send(source, target, k, bit):
            slot = len(sent)
            copy = pltpu.make_async_remote_copy(
                src_ref=source,
                dst_ref=target,
                send_sem=send_sem.at[it, slot],
                recv_sem=recv_sem.at[it, slot],
                device_id={"leaf": flip(k, bit)},
                device_id_type=MESH,
            )
            copy.start()
            sent.append(copy)
            return copy

        def share(first, count):
            place = total.at[it, pl.ds(first, count), mine]
            return [send(place, place, k, 0) for k in (3, 2, 1)]

        def launch(stage):
            bit = 2 * stage + 2
            count = upper - bit
            copies = [send(pends[stage].at[it], firsts[stage].at[it], 1, bit)]
            if count > 1:
                for k in (2, 3):
                    copies.append(send(
                        pends[stage].at[it, pl.ds(1, count - 1)],
                        others[stage].at[it, k - 2], k, bit))
            return copies

        opening = [
            send(pend0.at[it, pl.ds(1, upper - 1), quarter_of(flip(k, 0))],
                 recv_q.at[it, k - 1], k, 0)
            for k in (3, 2, 1)
        ]
        opening.append(send(pend0.at[it, 0], recv_a.at[it], 1, 0))
        state = {"round": 0, "copies": opening, "back": []}

        def advance():
            stage = state["round"] - 1
            if stage >= n_stage:
                return
            for copy in state["copies"]:
                copy.wait_recv()
            if stage < 0:
                for u in range(1, upper):
                    value = pend0[it, u, mine]
                    for k in range(3):
                        value = value + recv_q[it, k, u - 1]
                    if u == 1:
                        total[it, u, mine] = value
                    else:
                        pends[0][it, u - 2] = value
                if n_stage > 0:
                    state["copies"] = launch(0)
                state["back"] += share(1, 1)
                total[it, 0] = pend0[it, 0] + recv_a[it]
            else:
                bit = 2 * stage + 2
                for u in range(bit, upper):
                    value = pends[stage][it, u - bit] + firsts[stage][it, u - bit]
                    if u > bit:
                        for k in range(2):
                            value = value + others[stage][it, k, u - bit - 1]
                    if u < bit + 2:
                        total[it, u, mine] = value
                    else:
                        pends[stage + 1][it, u - bit - 2] = value
                if stage + 1 < n_stage:
                    state["copies"] = launch(stage + 1)
                state["back"] += share(bit, min(2, upper - bit))
            state["round"] += 1

        for b in range(blocks):
            span = slice(b * leaf_size, (b + 1) * leaf_size)
            coef[b] = nt_dot(probe[:, span], bases[:low, span])
        for level in range(local):
            per_node = 2 ** (level + 1)
            lanes = slice(level * rank, (level + 1) * rank)
            for q in range(blocks // per_node):
                node = coef[q * per_node, :, lanes]
                for b in range(q * per_node + 1, (q + 1) * per_node):
                    node = node + coef[b, :, lanes]
                value = scaled(node, level)
                for b in range(q * per_node, (q + 1) * per_node):
                    low_s[b, :, lanes] = value
        if it == 0:
            leaf_copy.wait()
        curve = jnp.zeros((columns, TILE), jnp.float32)
        norm = jnp.zeros((columns, TILE), jnp.float32)
        power = jnp.zeros((columns, TILE), jnp.float32)
        last = it + 1 == ITERS
        for b in range(blocks):
            span = slice(b * leaf_size, (b + 1) * leaf_size)
            field = nn_dot(probe[:, span], leaf[b]) + nn_dot(low_s[b], bases[:low, span])
            image[:, span] = field
            if last:
                for c in range(leaf_size // TILE):
                    at = b * leaf_size + c * TILE
                    curve = curve + dirn[:, at:at + TILE] * field[:, c * TILE:(c + 1) * TILE]
                    left = left_field[:, at:at + TILE]
                    norm = norm + left * left
            if b == blocks - 3:
                advance()
        for _ in range(n_stage):
            advance()

        def vector(k):
            return pltpu.make_async_remote_copy(
                src_ref=vec_out.at[it],
                dst_ref=vec_in.at[it, k],
                send_sem=vsend_sem.at[it, k],
                recv_sem=vrecv_sem.at[it, k],
                device_id={"leaf": (me + k) % n_dev},
                device_id_type=MESH,
            )

        def push(k, carry):
            vector(k).start()
            return carry

        def take(k, carry):
            vector(k).wait()
            return carry + vec_in[it, k]

        def publish():
            vec_out[it, 0:1, :] = row_of(curve)
            vec_out[it, 1:2, :] = row_of(norm)
            vec_out[it, 2:3, :] = row_of(power)
            vec_out[it, 3:8, :] = jnp.zeros((5, TILE), jnp.float32)
            lax.fori_loop(1, n_dev, push, 0)

        if last:
            shared = total[it, 0]
            products[...] = curve + 0.5 * shared * scaled(shared, local).astype(jnp.float32)
            own = jnp.zeros((quarter, rank), jnp.float32)
            for u in range(1, upper):
                held = total[it, u, mine]
                own = own + 0.5 ** (u - 1) * held * scaled(held, local + u).astype(jnp.float32)
            products[mine] = products[mine] + own
            curve = products[...]
            publish()
        for copy in state["back"]:
            copy.wait_recv()
        for u in range(upper):
            up_s[:, u * rank:(u + 1) * rank] = scaled(total[it, u], local + u)

        for b in range(blocks):
            span = slice(b * leaf_size, (b + 1) * leaf_size)
            field = image[:, span] + nn_dot(up_s[...], bases[low:, span])
            image[:, span] = field
            if not last:
                for c in range(leaf_size // TILE):
                    at = b * leaf_size + c * TILE
                    piece = field[:, c * TILE:(c + 1) * TILE]
                    away = dirn[:, at:at + TILE]
                    left = away if it == 0 else left_field[:, at:at + TILE]
                    curve = curve + away * piece
                    norm = norm + left * left
                    power = power + piece * piece
        if not last:
            publish()
        for copy in sent:
            copy.wait_send()
        sums = lax.fori_loop(1, n_dev, take, vec_out[it])
        curvature, norm_now, squares = sums[0:1], sums[1:2], sums[2:3]
        step_row = norm_now / curvature
        step = spread(step_row)
        if it + 1 < ITERS:
            norm_next = norm_now - 2.0 * step_row * curvature + step_row * step_row * squares
            ratio = spread(norm_next / norm_now)
            for c in range(tiles):
                lanes = slice(c * TILE, (c + 1) * TILE)
                away = dirn[:, lanes]
                if it == 0:
                    rs[:, lanes] = step * away
                    left = away - step * image[:, lanes]
                else:
                    rs[:, lanes] = rs[:, lanes] + step * away
                    left = left_field[:, lanes] - step * image[:, lanes]
                left_field[:, lanes] = left
                fresh = left + ratio * away
                dirn[:, lanes] = fresh
                probe[:, lanes] = fresh.astype(jnp.bfloat16)

    outs = []
    for q in range(CHUNKS):
        for c in range(q * tiles // CHUNKS, (q + 1) * tiles // CHUNKS):
            lanes = slice(c * TILE, (c + 1) * TILE)
            srows[lanes, :] = (rs[:, lanes] + step * dirn[:, lanes]).T
            rst[lanes, :] = (left_field[:, lanes] - step * image[:, lanes]).T
        run = pl.ds(q * part, part)
        for n, (source, target) in enumerate(((srows, sol_hbm), (rst, res_hbm))):
            copy = pltpu.make_async_copy(source.at[run], target.at[run], out_sem.at[n, q])
            copy.start()
            outs.append(copy)
    for copy in outs:
        copy.wait()


def conjugate(right_side, point_order, leaf_blocks, bases, rank_weights, n_dev):
    columns, points = right_side.shape
    blocks, leaf_size, _ = leaf_blocks.shape
    levels, rank = rank_weights.shape
    upper = n_dev.bit_length() - 1
    local = levels - upper
    quarter = columns // 4
    starts = list(range(2, upper, 2))
    n_stage = len(starts)
    f32, bf16 = jnp.float32, jnp.bfloat16
    scratch = [
        pltpu.VMEM((columns, points), f32),
        pltpu.VMEM((points, columns), f32),
        pltpu.VMEM((TILE, columns), f32),
        pltpu.VMEM((points, columns), f32),
        pltpu.VMEM((blocks, leaf_size, leaf_size), bf16),
        pltpu.VMEM((levels * rank, points), bf16),
        pltpu.VMEM((columns, points), f32),
        pltpu.VMEM((columns, points), f32),
        pltpu.VMEM((columns, points), bf16),
        pltpu.VMEM((columns, points), f32),
        pltpu.VMEM((blocks, columns, local * rank), f32),
        pltpu.VMEM((blocks, columns, local * rank), bf16),
        pltpu.VMEM((columns, upper * rank), bf16),
        pltpu.VMEM((ITERS, upper, columns, rank), f32),
        pltpu.VMEM((ITERS, columns, rank), f32),
        pltpu.VMEM((ITERS, 3, upper - 1, quarter, rank), f32),
        pltpu.VMEM((ITERS, upper, columns, rank), f32),
        pltpu.VMEM((columns, rank), f32),
        pltpu.VMEM((ITERS, 8, columns), f32),
        pltpu.VMEM((ITERS, n_dev, 8, columns), f32),
    ]
    scratch += [pltpu.VMEM((ITERS, upper - b, quarter, rank), f32) for b in starts]
    scratch += [pltpu.VMEM((ITERS, upper - b, quarter, rank), f32) for b in starts]
    scratch += [pltpu.VMEM((ITERS, 2, max(upper - b - 1, 1), quarter, rank), f32) for b in starts]
    slots = 7 + 6 * n_stage
    scratch += [
        pltpu.SemaphoreType.DMA((CHUNKS,)),
        pltpu.SemaphoreType.DMA,
        pltpu.SemaphoreType.DMA,
        pltpu.SemaphoreType.DMA((ITERS, slots)),
        pltpu.SemaphoreType.DMA((ITERS, slots)),
        pltpu.SemaphoreType.DMA((ITERS, n_dev)),
        pltpu.SemaphoreType.DMA((ITERS, n_dev)),
        pltpu.SemaphoreType.DMA((2, CHUNKS)),
    ]
    hbm = pl.BlockSpec(memory_space=pl.ANY)
    vmem = pl.BlockSpec(memory_space=pltpu.VMEM)
    shape = jax.ShapeDtypeStruct((points, columns), f32)
    return pl.pallas_call(
        functools.partial(cg_kernel, n_dev, levels, n_stage),
        out_shape=(shape, shape),
        in_specs=[hbm, pl.BlockSpec(memory_space=pltpu.SMEM), hbm, hbm, vmem],
        out_specs=(hbm, hbm),
        scratch_shapes=scratch,
        compiler_params=pltpu.CompilerParams(
            collective_id=0, has_side_effects=True, vmem_limit_bytes=56 * 2 ** 20
        ),
        name="cg",
    )(right_side, point_order, leaf_blocks, bases.reshape(levels * rank, points), rank_weights)


def scatter_kernel(order_ref, sol_hbm, res_hbm, out_sol, out_res, sol_in, res_in, sol_rows, res_rows,
                   sol_turn, res_turn, in_sem, out_sem):
    points, columns = sol_in.shape
    tiles = points // TILE
    part = points // CHUNKS
    copies = []
    for q in range(CHUNKS):
        run = pl.ds(q * part, part)
        pair = []
        for n, (source, target) in enumerate(((sol_hbm, sol_in), (res_hbm, res_in))):
            copy = pltpu.make_async_copy(source.at[run], target.at[run], in_sem.at[n, q])
            copy.start()
            pair.append(copy)
        copies.append(pair)

    def place(c, carry):
        at = pl.multiple_of(c * TILE, TILE)
        for j in range(TILE):
            target = order_ref[at + j] & (points - 1)
            sol_rows[pl.ds(target, 1), :] = sol_in[pl.ds(at + j, 1), :]
            res_rows[pl.ds(target, 1), :] = res_in[pl.ds(at + j, 1), :]
        return carry

    for q in range(CHUNKS):
        for copy in copies[q]:
            copy.wait()
        lax.fori_loop(q * tiles // CHUNKS, (q + 1) * tiles // CHUNKS, place, 0)

    outs = []
    for q in range(CHUNKS):
        for c in range(q * tiles // CHUNKS, (q + 1) * tiles // CHUNKS):
            lanes = slice(c * TILE, (c + 1) * TILE)
            sol_turn[:, lanes] = sol_rows[lanes, :].T
            res_turn[:, lanes] = res_rows[lanes, :].T
        run = pl.ds(q * part, part)
        for n, (source, target) in enumerate(((sol_turn, out_sol), (res_turn, out_res))):
            copy = pltpu.make_async_copy(source.at[:, run], target.at[:, run], out_sem.at[n, q])
            copy.start()
            outs.append(copy)
    for copy in outs:
        copy.wait()


def scatter_back(point_order, field, residual):
    points, columns = field.shape
    hbm = pl.BlockSpec(memory_space=pl.ANY)
    shape = jax.ShapeDtypeStruct((columns, points), jnp.float32)
    return pl.pallas_call(
        scatter_kernel,
        out_shape=(shape, shape),
        in_specs=[pl.BlockSpec(memory_space=pltpu.SMEM), hbm, hbm],
        out_specs=(hbm, hbm),
        scratch_shapes=[pltpu.VMEM((points, columns), jnp.float32)] * 4
        + [pltpu.VMEM((columns, points), jnp.float32)] * 2
        + [pltpu.SemaphoreType.DMA((2, CHUNKS))] * 2,
        compiler_params=pltpu.CompilerParams(vmem_limit_bytes=56 * 2 ** 20),
        name="place",
    )(point_order, field, residual)


def on_device(right_side, point_order, leaf_blocks, bases, rank_weights, n_dev):
    field, residual = conjugate(right_side, point_order, leaf_blocks, bases, rank_weights, n_dev)
    return scatter_back(point_order, field, residual)


def solution(mesh):
    return jax.shard_map(
        functools.partial(on_device, n_dev=mesh.shape["leaf"]),
        mesh=mesh,
        in_specs=(
            P("groups", "leaf"),
            P(("groups", "leaf")),
            P("leaf", None, None),
            P(None, None, "leaf"),
            P(),
        ),
        out_specs=(P("groups", "leaf"), P("groups", "leaf")),
        check_vma=False,
    )
```

```python
import functools
import math

import jax
import jax.numpy as jnp
from jax import lax
from jax.experimental import pallas as pl
from jax.experimental.pallas import tpu as pltpu
from jax.sharding import PartitionSpec as P

ITERS = 2
TILE = 128
CHUNKS = 8
MESH = pl.DeviceIdType.MESH


def nt_dot(a, b):
    return lax.dot_general(a, b, (((1,), (1,)), ((), ())), preferred_element_type=jnp.float32)


def nn_dot(a, b):
    return jnp.dot(a, b, preferred_element_type=jnp.float32)


def row_of(matrix):
    return jnp.sum(matrix.T, axis=0, keepdims=True)


def spread(row):
    return jnp.broadcast_to(row, (TILE, row.shape[1])).T


def cg_kernel(n_dev, levels, n_stage, *refs):
    upper = n_dev.bit_length() - 1
    local = levels - upper
    refs = list(refs)

    def grab(count):
        taken = refs[:count]
        del refs[:count]
        return taken

    rs_hbm, order_ref, leaf_hbm, bases_hbm, weights_ref, sol_hbm, res_hbm = grab(7)
    rs, rst, rows, srows, leaf, bases, dirn, left_field, probe, image, coef, low_s, up_s = grab(13)
    pend0, recv_a, recv_q, total, products, vec_out, vec_in = grab(7)
    pends, firsts, others = grab(n_stage), grab(n_stage), grab(n_stage)
    rs_sem, leaf_sem, bases_sem, send_sem, recv_sem, vsend_sem, vrecv_sem, out_sem = grab(8)

    columns, points = rs.shape
    blocks, leaf_size = leaf.shape[0], leaf.shape[1]
    rank = weights_ref.shape[1]
    tiles = points // TILE
    quarter = columns // 4
    me = lax.axis_index("leaf")

    part = points // CHUNKS
    rs_copies = []
    for q in range(CHUNKS):
        lanes = pl.ds(q * part, part)
        copy = pltpu.make_async_copy(rs_hbm.at[:, lanes], rs.at[:, lanes], rs_sem.at[q])
        copy.start()
        rs_copies.append(copy)
    bases_copy = pltpu.make_async_copy(bases_hbm, bases, bases_sem)
    bases_copy.start()
    leaf_copy = pltpu.make_async_copy(leaf_hbm, leaf, leaf_sem)
    leaf_copy.start()

    barrier = pltpu.get_barrier_semaphore()

    def greet(k, carry):
        pl.semaphore_signal(
            barrier, inc=1, device_id={"leaf": (me + k) % n_dev}, device_id_type=MESH
        )
        return carry

    lax.fori_loop(1, n_dev, greet, 0)

    for q in range(CHUNKS):
        rs_copies[q].wait()
        for c in range(q * tiles // CHUNKS, (q + 1) * tiles // CHUNKS):
            at = c * TILE
            rst[at:at + TILE, :] = rs[:, at:at + TILE].T

    def fetch(at):
        for j in range(TILE):
            source = order_ref[at + j] & (points - 1)
            rows[pl.ds(j, 1), :] = rst[pl.ds(source, 1), :]

    def keep(at, tile):
        picked = tile.T
        dirn[:, pl.ds(at, TILE)] = picked
        probe[:, pl.ds(at, TILE)] = picked.astype(jnp.bfloat16)

    def fetch_keep(c, carry):
        at = pl.multiple_of(c * TILE, TILE)
        before = rows[...]
        fetch(at)
        keep(pl.multiple_of(at - TILE, TILE), before)
        return carry

    fetch(0)
    lax.fori_loop(1, tiles, fetch_keep, 0)
    keep(points - TILE, rows[...])

    def flip(k, bit):
        peer = me
        for step in range(2):
            if k >> step & 1:
                stride = 2 ** (bit + step)
                peer = peer + stride * (1 - 2 * ((me // stride) % 2))
        return peer

    def quarter_of(device):
        return pl.ds(pl.multiple_of(device % 4 * quarter, quarter), quarter)

    def scaled(values, level):
        factor = 1.0 / math.sqrt(rank * leaf_size * 2 ** (level + 1))
        return (values * factor * weights_ref[level:level + 1, :]).astype(jnp.bfloat16)

    mine = quarter_of(me)
    low = local * rank
    bases_copy.wait()

    for it in range(ITERS):
        up = nt_dot(probe[...], bases[low:, :])
        for u in range(upper):
            pend0[it, u] = up[:, u * rank:(u + 1) * rank]
        if it == 0:
            pl.semaphore_wait(barrier, n_dev - 1)
        sent = []

        def send(source, target, k, bit):
            slot = len(sent)
            copy = pltpu.make_async_remote_copy(
                src_ref=source,
                dst_ref=target,
                send_sem=send_sem.at[it, slot],
                recv_sem=recv_sem.at[it, slot],
                device_id={"leaf": flip(k, bit)},
                device_id_type=MESH,
            )
            copy.start()
            sent.append(copy)
            return copy

        def share(first, count):
            place = total.at[it, pl.ds(first, count), mine]
            return [send(place, place, k, 0) for k in (3, 2, 1)]

        def launch(stage):
            bit = 2 * stage + 2
            count = upper - bit
            copies = [send(pends[stage].at[it], firsts[stage].at[it], 1, bit)]
            if count > 1:
                for k in (2, 3):
                    copies.append(send(
                        pends[stage].at[it, pl.ds(1, count - 1)],
                        others[stage].at[it, k - 2], k, bit))
            return copies

        opening = [
            send(pend0.at[it, pl.ds(1, upper - 1), quarter_of(flip(k, 0))],
                 recv_q.at[it, k - 1], k, 0)
            for k in (3, 2, 1)
        ]
        opening.append(send(pend0.at[it, 0], recv_a.at[it], 1, 0))
        state = {"round": 0, "copies": opening, "back": []}

        def advance():
            stage = state["round"] - 1
            if stage >= n_stage:
                return
            for copy in state["copies"]:
                copy.wait_recv()
            if stage < 0:
                for u in range(1, upper):
                    value = pend0[it, u, mine]
                    for k in range(3):
                        value = value + recv_q[it, k, u - 1]
                    if u == 1:
                        total[it, u, mine] = value
                    else:
                        pends[0][it, u - 2] = value
                if n_stage > 0:
                    state["copies"] = launch(0)
                state["back"] += share(1, 1)
                total[it, 0] = pend0[it, 0] + recv_a[it]
            else:
                bit = 2 * stage + 2
                for u in range(bit, upper):
                    value = pends[stage][it, u - bit] + firsts[stage][it, u - bit]
                    if u > bit:
                        for k in range(2):
                            value = value + others[stage][it, k, u - bit - 1]
                    if u < bit + 2:
                        total[it, u, mine] = value
                    else:
                        pends[stage + 1][it, u - bit - 2] = value
                if stage + 1 < n_stage:
                    state["copies"] = launch(stage + 1)
                state["back"] += share(bit, min(2, upper - bit))
            state["round"] += 1

        for b in range(blocks):
            span = slice(b * leaf_size, (b + 1) * leaf_size)
            coef[b] = nt_dot(probe[:, span], bases[:low, span])
        for level in range(local):
            per_node = 2 ** (level + 1)
            lanes = slice(level * rank, (level + 1) * rank)
            for q in range(blocks // per_node):
                node = coef[q * per_node, :, lanes]
                for b in range(q * per_node + 1, (q + 1) * per_node):
                    node = node + coef[b, :, lanes]
                value = scaled(node, level)
                for b in range(q * per_node, (q + 1) * per_node):
                    low_s[b, :, lanes] = value
        if it == 0:
            leaf_copy.wait()
        curve = jnp.zeros((columns, TILE), jnp.float32)
        norm = jnp.zeros((columns, TILE), jnp.float32)
        power = jnp.zeros((columns, TILE), jnp.float32)
        last = it + 1 == ITERS
        for b in range(blocks):
            span = slice(b * leaf_size, (b + 1) * leaf_size)
            field = nn_dot(probe[:, span], leaf[b]) + nn_dot(low_s[b], bases[:low, span])
            image[:, span] = field
            if last:
                for c in range(leaf_size // TILE):
                    at = b * leaf_size + c * TILE
                    curve = curve + dirn[:, at:at + TILE] * field[:, c * TILE:(c + 1) * TILE]
                    left = left_field[:, at:at + TILE]
                    norm = norm + left * left
            if b == blocks - 3:
                advance()
        for _ in range(n_stage):
            advance()

        def vector(k):
            return pltpu.make_async_remote_copy(
                src_ref=vec_out.at[it],
                dst_ref=vec_in.at[it, k],
                send_sem=vsend_sem.at[it, k],
                recv_sem=vrecv_sem.at[it, k],
                device_id={"leaf": (me + k) % n_dev},
                device_id_type=MESH,
            )

        def push(k, carry):
            vector(k).start()
            return carry

        def take(k, carry):
            vector(k).wait()
            return carry + vec_in[it, k]

        def publish():
            vec_out[it, 0:1, :] = row_of(curve)
            vec_out[it, 1:2, :] = row_of(norm)
            vec_out[it, 2:3, :] = row_of(power)
            vec_out[it, 3:8, :] = jnp.zeros((5, TILE), jnp.float32)
            lax.fori_loop(1, n_dev, push, 0)

        if last:
            shared = total[it, 0]
            products[...] = curve + 0.5 * shared * scaled(shared, local).astype(jnp.float32)
            own = jnp.zeros((quarter, rank), jnp.float32)
            for u in range(1, upper):
                held = total[it, u, mine]
                own = own + 0.5 ** (u - 1) * held * scaled(held, local + u).astype(jnp.float32)
            products[mine] = products[mine] + own
            curve = products[...]
            publish()
        for copy in state["back"]:
            copy.wait_recv()
        for u in range(upper):
            up_s[:, u * rank:(u + 1) * rank] = scaled(total[it, u], local + u)

        for b in range(blocks):
            span = slice(b * leaf_size, (b + 1) * leaf_size)
            field = image[:, span] + nn_dot(up_s[...], bases[low:, span])
            image[:, span] = field
            if not last:
                for c in range(leaf_size // TILE):
                    at = b * leaf_size + c * TILE
                    piece = field[:, c * TILE:(c + 1) * TILE]
                    away = dirn[:, at:at + TILE]
                    left = away if it == 0 else left_field[:, at:at + TILE]
                    curve = curve + away * piece
                    norm = norm + left * left
                    power = power + piece * piece
        if not last:
            publish()
        for copy in sent:
            copy.wait_send()
        sums = lax.fori_loop(1, n_dev, take, vec_out[it])
        curvature, norm_now, squares = sums[0:1], sums[1:2], sums[2:3]
        step_row = norm_now / curvature
        step = spread(step_row)
        if it + 1 < ITERS:
            norm_next = norm_now - 2.0 * step_row * curvature + step_row * step_row * squares
            ratio = spread(norm_next / norm_now)
            for c in range(tiles):
                lanes = slice(c * TILE, (c + 1) * TILE)
                away = dirn[:, lanes]
                if it == 0:
                    rs[:, lanes] = step * away
                    left = away - step * image[:, lanes]
                else:
                    rs[:, lanes] = rs[:, lanes] + step * away
                    left = left_field[:, lanes] - step * image[:, lanes]
                left_field[:, lanes] = left
                fresh = left + ratio * away
                dirn[:, lanes] = fresh
                probe[:, lanes] = fresh.astype(jnp.bfloat16)

    outs = []
    for q in range(CHUNKS):
        for c in range(q * tiles // CHUNKS, (q + 1) * tiles // CHUNKS):
            lanes = slice(c * TILE, (c + 1) * TILE)
            srows[lanes, :] = (rs[:, lanes] + step * dirn[:, lanes]).T
            rst[lanes, :] = (left_field[:, lanes] - step * image[:, lanes]).T
        run = pl.ds(q * part, part)
        for n, (source, target) in enumerate(((srows, sol_hbm), (rst, res_hbm))):
            copy = pltpu.make_async_copy(source.at[run], target.at[run], out_sem.at[n, q])
            copy.start()
            outs.append(copy)
    for copy in outs:
        copy.wait()


def conjugate(right_side, point_order, leaf_blocks, bases, rank_weights, n_dev):
    columns, points = right_side.shape
    blocks, leaf_size, _ = leaf_blocks.shape
    levels, rank = rank_weights.shape
    upper = n_dev.bit_length() - 1
    local = levels - upper
    quarter = columns // 4
    starts = list(range(2, upper, 2))
    n_stage = len(starts)
    f32, bf16 = jnp.float32, jnp.bfloat16
    scratch = [
        pltpu.VMEM((columns, points), f32),
        pltpu.VMEM((points, columns), f32),
        pltpu.VMEM((TILE, columns), f32),
        pltpu.VMEM((points, columns), f32),
        pltpu.VMEM((blocks, leaf_size, leaf_size), bf16),
        pltpu.VMEM((levels * rank, points), bf16),
        pltpu.VMEM((columns, points), f32),
        pltpu.VMEM((columns, points), f32),
        pltpu.VMEM((columns, points), bf16),
        pltpu.VMEM((columns, points), f32),
        pltpu.VMEM((blocks, columns, local * rank), f32),
        pltpu.VMEM((blocks, columns, local * rank), bf16),
        pltpu.VMEM((columns, upper * rank), bf16),
        pltpu.VMEM((ITERS, upper, columns, rank), f32),
        pltpu.VMEM((ITERS, columns, rank), f32),
        pltpu.VMEM((ITERS, 3, upper - 1, quarter, rank), f32),
        pltpu.VMEM((ITERS, upper, columns, rank), f32),
        pltpu.VMEM((columns, rank), f32),
        pltpu.VMEM((ITERS, 8, columns), f32),
        pltpu.VMEM((ITERS, n_dev, 8, columns), f32),
    ]
    scratch += [pltpu.VMEM((ITERS, upper - b, quarter, rank), f32) for b in starts]
    scratch += [pltpu.VMEM((ITERS, upper - b, quarter, rank), f32) for b in starts]
    scratch += [pltpu.VMEM((ITERS, 2, max(upper - b - 1, 1), quarter, rank), f32) for b in starts]
    slots = 7 + 6 * n_stage
    scratch += [
        pltpu.SemaphoreType.DMA((CHUNKS,)),
        pltpu.SemaphoreType.DMA,
        pltpu.SemaphoreType.DMA,
        pltpu.SemaphoreType.DMA((ITERS, slots)),
        pltpu.SemaphoreType.DMA((ITERS, slots)),
        pltpu.SemaphoreType.DMA((ITERS, n_dev)),
        pltpu.SemaphoreType.DMA((ITERS, n_dev)),
        pltpu.SemaphoreType.DMA((2, CHUNKS)),
    ]
    hbm = pl.BlockSpec(memory_space=pl.ANY)
    vmem = pl.BlockSpec(memory_space=pltpu.VMEM)
    shape = jax.ShapeDtypeStruct((points, columns), f32)
    return pl.pallas_call(
        functools.partial(cg_kernel, n_dev, levels, n_stage),
        out_shape=(shape, shape),
        in_specs=[hbm, pl.BlockSpec(memory_space=pltpu.SMEM), hbm, hbm, vmem],
        out_specs=(hbm, hbm),
        scratch_shapes=scratch,
        compiler_params=pltpu.CompilerParams(
            collective_id=0, has_side_effects=True, vmem_limit_bytes=56 * 2 ** 20
        ),
        name="cg",
    )(right_side, point_order, leaf_blocks, bases.reshape(levels * rank, points), rank_weights)


def scatter_kernel(order_ref, sol_hbm, res_hbm, out_sol, out_res, sol_in, res_in, sol_rows, res_rows,
                   sol_turn, res_turn, in_sem, out_sem):
    points, columns = sol_in.shape
    tiles = points // TILE
    part = points // CHUNKS
    copies = []
    for q in range(CHUNKS):
        run = pl.ds(q * part, part)
        pair = []
        for n, (source, target) in enumerate(((sol_hbm, sol_in), (res_hbm, res_in))):
            copy = pltpu.make_async_copy(source.at[run], target.at[run], in_sem.at[n, q])
            copy.start()
            pair.append(copy)
        copies.append(pair)

    def place(c, carry):
        at = pl.multiple_of(c * TILE, TILE)
        for j in range(TILE):
            target = order_ref[at + j] & (points - 1)
            sol_rows[pl.ds(target, 1), :] = sol_in[pl.ds(at + j, 1), :]
            res_rows[pl.ds(target, 1), :] = res_in[pl.ds(at + j, 1), :]
        return carry

    for q in range(CHUNKS):
        for copy in copies[q]:
            copy.wait()
        lax.fori_loop(q * tiles // CHUNKS, (q + 1) * tiles // CHUNKS, place, 0)

    outs = []
    for q in range(CHUNKS):
        for c in range(q * tiles // CHUNKS, (q + 1) * tiles // CHUNKS):
            lanes = slice(c * TILE, (c + 1) * TILE)
            sol_turn[:, lanes] = sol_rows[lanes, :].T
            res_turn[:, lanes] = res_rows[lanes, :].T
        run = pl.ds(q * part, part)
        for n, (source, target) in enumerate(((sol_turn, out_sol), (res_turn, out_res))):
            copy = pltpu.make_async_copy(source.at[:, run], target.at[:, run], out_sem.at[n, q])
            copy.start()
            outs.append(copy)
    for copy in outs:
        copy.wait()


def scatter_back(point_order, field, residual):
    points, columns = field.shape
    hbm = pl.BlockSpec(memory_space=pl.ANY)
    shape = jax.ShapeDtypeStruct((columns, points), jnp.float32)
    return pl.pallas_call(
        scatter_kernel,
        out_shape=(shape, shape),
        in_specs=[pl.BlockSpec(memory_space=pltpu.SMEM), hbm, hbm],
        out_specs=(hbm, hbm),
        scratch_shapes=[pltpu.VMEM((points, columns), jnp.float32)] * 4
        + [pltpu.VMEM((columns, points), jnp.float32)] * 2
        + [pltpu.SemaphoreType.DMA((2, CHUNKS))] * 2,
        compiler_params=pltpu.CompilerParams(vmem_limit_bytes=56 * 2 ** 20),
        name="place",
    )(point_order, field, residual)


def on_device(right_side, point_order, leaf_blocks, bases, rank_weights, n_dev):
    field, residual = conjugate(right_side, point_order, leaf_blocks, bases, rank_weights, n_dev)
    return scatter_back(point_order, field, residual)


def solution(mesh):
    return jax.shard_map(
        functools.partial(on_device, n_dev=mesh.shape["leaf"]),
        mesh=mesh,
        in_specs=(
            P("groups", "leaf"),
            P(("groups", "leaf")),
            P("leaf", None, None),
            P(None, None, "leaf"),
            P(),
        ),
        out_specs=(P("groups", "leaf"), P("groups", "leaf")),
        check_vma=False,
    )
```
